32 devices in a mesh: ctx: 8 (over z, y), rep: 4 (over x, core).
Axes of the slice: x: 2, y: 2, z: 4, core: 2. Of those that a mesh axis runs over, the one named last changes fastest.
Arguments:
- queries: bfloat16 [4096, 1024], P(('rep', 'ctx')), parts along dimension 0, may hold values from -6 to 6
- key_rows: bfloat16 [4096, 1024], P(('rep', 'ctx')), parts along dimension 0, may hold values from -6 to 6
- value_rows: bfloat16 [4096, 1024], P(('rep', 'ctx')), parts along dimension 0, may hold values from -8 to 8
- doc_blocks: int32 [12], P('rep'), parts along dimension 0, may hold values from 1 to 4, 8 in all
- phm_mix: float32 [4, 4, 4], replicated, may hold values from -4 to 4
- phm_blocks: bfloat16 [1024, 1280], P('ctx'), may hold values from -0.1875 to 0.1875
Outputs:
- projected: bfloat16 [4096, 5120], P(('rep', 'ctx')), parts along dimension 0
The draws below stay inside these ranges and needn't reach their ends.
There are 4 independent parts, one for each index of `rep`. The reference program is written for one: setup_inputs(seed, part) draws one part's arguments, and reference() takes and returns one part's arrays. A program takes and returns all parts, laid end to end along the dimension named above; an argument that names none is the same for every part. Nothing has to cross between parts.
Inputs may be any that keep to these rules, and one draw needn't show every extreme that they name: `doc_blocks`: entries sum to 8; the largest entry is exactly 4.
All inputs are finite; a program needn't handle non-finite values.
Results may differ from the reference program's by a relative error of at most 0.006.
Values may be sent and summed in bfloat16 or wider, within the bound.
A program may use at most 64 MiB of HBM per device.

```python
import math
import jax
import jax.numpy as jnp
import numpy as np
from jax import lax

HEAD_DIM = 128
PHM_N = 4
UNIT = 128
HEADS = 8
SEQ = 1024
DOC_MOST = 512
DOCS = 3
ROWS_PHM = 256
COLS_PHM = 1280


def drawn_pair(key):
    base = jax.random.fold_in(key, 17)
    key_first, key_second = jax.random.split(base, 2)
    width = HEADS * HEAD_DIM
    first = 1.4 * jax.random.truncated_normal(key_first, -4.2, 4.2, (SEQ, width), jnp.float32)
    second = 1.4 * jax.random.truncated_normal(key_second, -4.2, 4.2, (SEQ, width), jnp.float32)
    return (first, second)


def draw_queries(key, part):
    return drawn_pair(key)[0].astype(jnp.bfloat16)


def draw_key_rows(key, part):
    return drawn_pair(key)[1].astype(jnp.bfloat16)


def level_of(stream_key, dims, shards, least, largest):
    def one(dim, shards_of):
        steps = jax.random.uniform(jax.random.fold_in(jax.random.fold_in(stream_key, 6), dim), (shards_of,), jnp.float32, least / len(shards), largest / len(shards))
        return jnp.repeat(jnp.exp(steps), dims[dim] // shards_of).reshape((-1,) + (1,) * (len(dims) - dim - 1))

    loudness = one(*shards[0])
    for cut in shards[1:]:
        loudness = loudness * one(*cut)
    return loudness


def split_up(count, total, most, lean):
    portions = [(1 << 20) // math.isqrt(rank ** lean) + 1 for rank in range(2, count + 1)]
    surplus, counts = total - most - (count - 1), [1] * (count - 1)
    while surplus > 0:
        candidates = [i for i in range(count - 1) if counts[i] < most]
        whole, budget = sum([portions[i] for i in candidates]), surplus
        for i in candidates:
            extra = min(most - counts[i], max(1, budget * portions[i] // whole), surplus)
            counts[i] = counts[i] + extra
            surplus = surplus - extra
    return np.array([most] + counts)


def ragged(stream_key, count, total, reach, slope):
    if count == 2:
        one = jax.random.randint(stream_key, (), max(1, total - reach), min(reach, total - 1) + 1)
        return jnp.stack([one, total - one])
    sizes = jnp.asarray(split_up(count, total, reach, slope), jnp.int32)
    pairs = (count - 1) // 2
    giver, receiver = sizes[1:1 + 2 * pairs:2], sizes[2:2 + 2 * pairs:2]
    room = jnp.minimum(giver - 1, reach - receiver)
    shifted = jax.random.randint(jax.random.fold_in(stream_key, 1), (pairs,), 0, 1 << 20) % (room + 1)
    sizes = sizes.at[1:1 + 2 * pairs:2].set(giver - shifted).at[2:2 + 2 * pairs:2].set(receiver + shifted)
    return sizes[jax.random.permutation(jax.random.fold_in(stream_key, 2), count)]


def bell_draw(stream_key, dims, spread, bound, shards=(), kind=jnp.bfloat16):
    values = spread * jax.random.normal(stream_key, dims, jnp.float32)
    if shards:
        values = values * level_of(stream_key, dims, shards, -0.22, 0.18)
    return jnp.clip(values, -bound, bound).astype(kind)


def setup_inputs(seed: int = 0, part: int = 0) -> dict:
    seeds = jax.random.split(jax.random.key(seed), 7)
    part_keys = jax.random.split(jax.random.fold_in(seeds[6], part), 7)
    return {
        "queries": draw_queries(jax.random.fold_in(jax.random.fold_in(seeds[6], part), 71), part),
        "key_rows": draw_key_rows(jax.random.fold_in(jax.random.fold_in(seeds[6], part), 71), part),
        "value_rows": bell_draw(part_keys[2], (SEQ, HEADS * HEAD_DIM), 2.0, 8.0, ((0, 8),)),
        "doc_blocks": ragged(part_keys[3], DOCS, SEQ // UNIT, DOC_MOST // UNIT, 2).astype(jnp.int32),
        "phm_mix": bell_draw(seeds[4], (PHM_N, PHM_N, PHM_N), 1.0, 4.0, (), jnp.float32),
        "phm_blocks": bell_draw(seeds[5], (PHM_N * ROWS_PHM, COLS_PHM), (PHM_N * ROWS_PHM) ** -0.5, 0.1875, ((0, 8),)),
    }


def reference(queries, key_rows, value_rows, doc_blocks, phm_mix, phm_blocks):
    seq_len = queries.shape[0]
    ends = jnp.cumsum(doc_blocks.astype(jnp.int32) * UNIT).astype(jnp.int32)
    positions = jnp.arange(seq_len, dtype=jnp.int32)
    doc_ids = lax.optimization_barrier(jnp.sum((positions[:, None] >= ends[None, :]).astype(jnp.int32), axis=1))
    allowed = (positions[None, :] <= positions[:, None]) & (doc_ids[None, :] == doc_ids[:, None])
    scale = 1.0 / math.sqrt(HEAD_DIM)
    heads = queries.shape[1] // HEAD_DIM
    q_heads = queries.reshape(seq_len, heads, HEAD_DIM).transpose(1, 0, 2)
    k_heads = key_rows.reshape(seq_len, heads, HEAD_DIM).transpose(1, 0, 2)
    v_heads = value_rows.reshape(seq_len, heads, HEAD_DIM).transpose(1, 0, 2)

    def one_head(operands):
        q_one, k_one, v_one = operands
        scores = jnp.dot(q_one, k_one.T, preferred_element_type=jnp.float32) * scale
        scores = jnp.where(allowed, scores, -jnp.inf)
        row_max = lax.optimization_barrier(jnp.max(scores, axis=1, keepdims=True))
        expd = jnp.where(allowed, jnp.exp(scores - row_max), 0.0)
        totals = lax.optimization_barrier(jnp.sum(expd, axis=1, keepdims=True))
        probs = expd.astype(jnp.bfloat16)
        attended = jnp.dot(probs, v_one, preferred_element_type=jnp.float32) / totals
        return attended.astype(jnp.bfloat16)
    attended = lax.map(one_head, (q_heads, k_heads, v_heads))
    attended = attended.transpose(1, 0, 2).reshape(seq_len, heads * HEAD_DIM)
    rows_phm = heads * HEAD_DIM // PHM_N
    pieces = attended.reshape(seq_len, PHM_N, rows_phm).astype(jnp.float32)
    mixed = jnp.einsum('iab,tar->tbir', phm_mix.astype(jnp.float32), pieces, precision=lax.Precision.HIGHEST)
    mixed = mixed.astype(jnp.bfloat16).reshape(seq_len, PHM_N, PHM_N * rows_phm)
    result = jnp.einsum('tbk,kc->tbc', mixed.astype(jnp.float32), phm_blocks.astype(jnp.float32))
    return result.reshape(seq_len, PHM_N * phm_blocks.shape[1]).astype(jnp.bfloat16)
```

```python
import functools
import math

import jax
import jax.numpy as jnp
from jax import lax
from jax.experimental import pallas as pl
from jax.experimental.pallas import tpu as pltpu
from jax.sharding import PartitionSpec as P

HEAD_DIM = 128
PHM_N = 4
UNIT = 128


def attend(q_all, k_all, v_all, doc_ids):
    seq_len = q_all.shape[0]
    block = min(512, seq_len)
    count = seq_len // block
    scale = 1.0 / math.sqrt(HEAD_DIM)
    heads_here = q_all.shape[1]

    def query_block(which):
        anchor = which * block
        q_part = lax.dynamic_slice_in_dim(q_all, anchor, block, 0)
        q_docs = lax.dynamic_slice_in_dim(doc_ids, anchor, block, 0)
        q_pos = anchor + jnp.arange(block, dtype=jnp.int32)
        lowest = jnp.int32(0)

        def key_block(kb, carry):
            running, total, accum = carry
            k_part = lax.dynamic_slice_in_dim(k_all, kb * block, block, 0)
            v_part = lax.dynamic_slice_in_dim(v_all, kb * block, block, 0)
            k_docs = lax.dynamic_slice_in_dim(doc_ids, kb * block, block, 0)
            k_pos = kb * block + jnp.arange(block, dtype=jnp.int32)
            allowed = (k_pos[None, :] <= q_pos[:, None]) & (k_docs[None, :] == q_docs[:, None])
            scores = (
                jnp.einsum("qhe,khe->hqk", q_part, k_part, preferred_element_type=jnp.float32)
                * scale
            )
            scores = jnp.where(allowed[None], scores, -1e30)
            newest = jnp.maximum(running, jnp.max(scores, axis=2))
            factor = jnp.exp(running - newest)
            expd = jnp.where(allowed[None], jnp.exp(scores - newest[:, :, None]), 0.0)
            total = total * factor + jnp.sum(expd, axis=2)
            update = jnp.einsum(
                "hqk,khe->hqe",
                expd.astype(jnp.bfloat16),
                v_part,
                preferred_element_type=jnp.float32,
            )
            accum = accum * factor[:, :, None] + update
            return (newest, total, accum)

        start_carry = (
            jnp.full((heads_here, block), -1e30, jnp.float32),
            jnp.zeros((heads_here, block), jnp.float32),
            jnp.zeros((heads_here, block, HEAD_DIM), jnp.float32),
        )
        running, total, accum = lax.fori_loop(lowest, which + 1, key_block, start_carry)
        result = (accum / total[:, :, None]).astype(jnp.bfloat16)
        return result.transpose(1, 0, 2)

    blocks_out = lax.map(query_block, jnp.arange(count, dtype=jnp.int32))
    return blocks_out.reshape(seq_len, heads_here, HEAD_DIM)


def body(queries, key_rows, value_rows, doc_blocks, phm_mix, phm_blocks):
    tok_rows = queries.shape[0]
    heads = queries.shape[1] // HEAD_DIM
    shaped = (
        queries.reshape(tok_rows, heads, HEAD_DIM),
        key_rows.reshape(tok_rows, heads, HEAD_DIM),
        value_rows.reshape(tok_rows, heads, HEAD_DIM),
    )
    q_all, k_all, v_all = (
        lax.all_to_all(shaped[0], "ctx", split_axis=1, concat_axis=0, tiled=True),
        lax.all_to_all(shaped[1], "ctx", split_axis=1, concat_axis=0, tiled=True),
        lax.all_to_all(shaped[2], "ctx", split_axis=1, concat_axis=0, tiled=True),
    )
    seq_len = q_all.shape[0]
    lengths = doc_blocks * UNIT
    ends = jnp.cumsum(lengths)
    positions = jnp.arange(seq_len, dtype=jnp.int32)
    doc_ids = jnp.sum((positions[:, None] >= ends[None, :]).astype(jnp.int32), axis=1)
    attended = attend(q_all, k_all, v_all, doc_ids)
    returned = lax.all_to_all(attended, "ctx", split_axis=0, concat_axis=1, tiled=True)
    rows_phm = heads * HEAD_DIM // PHM_N
    pieces = returned.reshape(tok_rows, PHM_N, rows_phm).astype(jnp.float32)
    mixed = jnp.einsum("iab,tar->tbir", phm_mix, pieces, precision=lax.Precision.HIGHEST)
    mixed = mixed.astype(jnp.bfloat16).reshape(tok_rows, PHM_N, PHM_N * rows_phm)
    cols_phm = phm_blocks.shape[1]
    output = jnp.einsum(
        "tbk,kc->tbc",
        mixed,
        lax.all_gather(phm_blocks, "ctx", axis=0, tiled=True),
        preferred_element_type=jnp.float32,
    )
    return output.reshape(tok_rows, PHM_N * cols_phm).astype(jnp.bfloat16)


MESH = pl.DeviceIdType.MESH
ROWS = UNIT
MASKED = -1e30


def fused_kernel(
    docs_ref, mix_ref, q_ref, k_ref, v_ref, w_ref, out_ref,
    qkv, obuf, att, wbuf, mixed,
    qkv_send, qkv_recv, o_send, o_recv, w_send, w_recv, own_sem,
):
    ctx = 8
    window = 4
    d = lax.axis_index("ctx")
    r = lax.axis_index("rep")
    z = d // 2
    y_peer = d + 1 - 2 * (d % 2)
    x_peer = (r + 2) % 4
    c_peer = r + 1 - 2 * (r % 2)
    part = ROWS // 4

    barrier = pltpu.get_barrier_semaphore()
    for off in range(1, ctx):
        pl.semaphore_signal(
            barrier, inc=1, device_id={"ctx": (d + off) % ctx}, device_id_type=MESH
        )
    for peer in (x_peer, c_peer):
        pl.semaphore_signal(barrier, inc=1, device_id={"rep": peer}, device_id_type=MESH)
    pl.semaphore_wait(barrier, ctx + 1)

    def quarter(shard, which):
        return wbuf.at[shard, pl.ds(pl.multiple_of(which * part, part), part)]

    def w_copy(src, shard, which, way, target):
        return pltpu.make_async_remote_copy(
            src_ref=src,
            dst_ref=quarter(shard, which),
            send_sem=w_send.at[way, shard, which],
            recv_sem=w_recv.at[shard, which],
            device_id=target,
            device_id_type=MESH,
        )

    def w_arrived(shard, which):
        here = quarter(shard, which)
        pltpu.make_async_copy(here, here, w_recv.at[shard, which]).wait()

    def w_sent(shard, which, way):
        here = quarter(shard, which)
        pltpu.make_async_copy(here, here, w_send.at[way, shard, which]).wait()

    own_w = w_ref.at[pl.ds(pl.multiple_of(r * part, part), part)]

    @pl.when(z < 3)
    def _():
        w_copy(own_w, d, r, 0, {"ctx": d + 2}).start()

    @pl.when(z > 0)
    def _():
        w_copy(own_w, d, r, 1, {"ctx": d - 2}).start()

    w_copy(own_w, d, r, 2, {"ctx": y_peer}).start()

    refs = (q_ref, k_ref, v_ref)

    def head_copy(j, to):
        return pltpu.make_async_remote_copy(
            src_ref=refs[j].at[:, pl.ds(pl.multiple_of(to * HEAD_DIM, HEAD_DIM), HEAD_DIM)],
            dst_ref=qkv.at[j, d],
            send_sem=qkv_send.at[j, to],
            recv_sem=qkv_recv.at[j, d],
            device_id={"ctx": to},
            device_id_type=MESH,
        )

    for off in (4, 5, 3, 6, 2, 7, 1):
        for j in range(3):
            head_copy(j, (d + off) % ctx).start()
    for j in range(3):
        pltpu.make_async_copy(
            refs[j].at[:, pl.ds(pl.multiple_of(d * HEAD_DIM, HEAD_DIM), HEAD_DIM)],
            qkv.at[j, d],
            qkv_recv.at[j, d],
        ).start()
    own_copy = pltpu.make_async_copy(w_ref, wbuf.at[d], own_sem)
    own_copy.start()

    def forward(shard, which, way, target):
        w_copy(quarter(shard, which), shard, which, way, target).start()

    for k in range(1, 4):

        @pl.when(z - k >= 0)
        def _():
            shard = d - 2 * k
            w_arrived(shard, r)

            @pl.when(z < 3)
            def _():
                forward(shard, r, 0, {"ctx": d + 2})

            forward(shard, r, 2, {"ctx": y_peer})
            forward(shard, r, 3, {"rep": x_peer})
            forward(shard, r, 4, {"rep": c_peer})

        @pl.when(z + k <= 3)
        def _():
            shard = d + 2 * k
            w_arrived(shard, r)

            @pl.when(z > 0)
            def _():
                forward(shard, r, 1, {"ctx": d - 2})

            forward(shard, r, 2, {"ctx": y_peer})
            forward(shard, r, 3, {"rep": x_peer})
            forward(shard, r, 4, {"rep": c_peer})

    for k in range(4):
        shard = (y_peer + 2 * k) % ctx
        w_arrived(shard, r)
        forward(shard, r, 3, {"rep": x_peer})
        forward(shard, r, 4, {"rep": c_peer})

    ends = [docs_ref[0]]
    for i in range(1, docs_ref.shape[0]):
        ends.append(ends[-1] + docs_ref[i])
    ids = []
    for b in range(ctx):
        doc = jnp.int32(0)
        for e in ends:
            doc = doc + jnp.where(e <= b, jnp.int32(1), jnp.int32(0))
        ids.append(doc)
    factor = math.log2(math.e) / math.sqrt(HEAD_DIM)
    rows = lax.broadcasted_iota(jnp.int32, (ROWS, ROWS), 0)
    cols = lax.broadcasted_iota(jnp.int32, (ROWS, ROWS), 1)

    def o_copy(b):
        return pltpu.make_async_remote_copy(
            src_ref=obuf.at[b],
            dst_ref=att.at[d],
            send_sem=o_send.at[b],
            recv_sem=o_recv.at[d],
            device_id={"ctx": b},
            device_id_type=MESH,
        )

    for b in range(ctx):
        for j in range(3):
            here = qkv.at[j, b]
            pltpu.make_async_copy(here, here, qkv_recv.at[j, b]).wait()
        low = max(0, b - window + 1)
        wide = (b + 1 - low) * ROWS
        keys = qkv[1, low : b + 1].reshape(wide, HEAD_DIM)
        vals = qkv[2, low : b + 1].reshape(wide, HEAD_DIM)
        scores = lax.dot_general(
            qkv[0, b], keys, (((1,), (1,)), ((), ())), preferred_element_type=jnp.float32
        )
        parts = []
        for kb in range(low, b + 1):
            one = scores[:, (kb - low) * ROWS : (kb - low + 1) * ROWS]
            if kb == b:
                one = jnp.where(cols <= rows, one, MASKED)
            else:
                one = one + jnp.where(ids[kb] == ids[b], 0.0, MASKED)
            parts.append(one)
        masked = jnp.concatenate(parts, axis=1) if len(parts) > 1 else parts[0]
        top = jnp.max(masked, axis=1, keepdims=True)
        expd = jnp.exp2((masked - top) * factor)
        total = jnp.sum(expd, axis=1, keepdims=True)
        got = jnp.dot(expd.astype(jnp.bfloat16), vals, preferred_element_type=jnp.float32)
        obuf[b] = (got / total).astype(jnp.bfloat16)

        @pl.when(d != b)
        def _():
            o_copy(b).start()

        @pl.when(d == b)
        def _():
            pltpu.make_async_copy(obuf.at[b], att.at[d], o_recv.at[d]).start()

    for off in range(1, ctx):
        shard = (d + off) % ctx
        w_arrived(shard, x_peer)
        forward(shard, x_peer, 4, {"rep": c_peer})

    for h in range(ctx):
        here = att.at[h]
        pltpu.make_async_copy(here, here, o_recv.at[h]).wait()

    for half in range(2):
        pieces = [att[2 * a + half].astype(jnp.float32) for a in range(PHM_N)]
        for i in range(PHM_N):
            for b in range(PHM_N):
                acc = mix_ref[(i * PHM_N + 0) * PHM_N + b] * pieces[0]
                for a in range(1, PHM_N):
                    acc = acc + mix_ref[(i * PHM_N + a) * PHM_N + b] * pieces[a]
                lo = i * 2 * HEAD_DIM + half * HEAD_DIM
                mixed[b * ROWS : (b + 1) * ROWS, lo : lo + HEAD_DIM] = acc.astype(jnp.bfloat16)

    own_copy.wait()
    x_of_c = (c_peer + 2) % 4
    for off in range(1, ctx):
        shard = (d + off) % ctx
        w_arrived(shard, c_peer)
        w_arrived(shard, x_of_c)

    cols_phm = w_ref.shape[1]
    tile = 256
    for c in range(cols_phm // tile):
        weights = wbuf[:, :, c * tile : (c + 1) * tile].reshape(ctx * ROWS, tile)
        res = jnp.dot(mixed[...], weights, preferred_element_type=jnp.float32)
        res = res.astype(jnp.bfloat16)
        for b in range(PHM_N):
            at = b * cols_phm + c * tile
            out_ref[:, at : at + tile] = res[b * ROWS : (b + 1) * ROWS]

    for off in range(1, ctx):
        for j in range(3):
            head_copy(j, (d + off) % ctx).wait_send()
    for b in range(ctx):

        @pl.when(d != b)
        def _():
            o_copy(b).wait_send()

    @pl.when(z < 3)
    def _():
        w_sent(d, r, 0)

    @pl.when(z > 0)
    def _():
        w_sent(d, r, 1)

    w_sent(d, r, 2)
    for k in range(1, 4):

        @pl.when(z - k >= 0)
        def _():
            shard = d - 2 * k

            @pl.when(z < 3)
            def _():
                w_sent(shard, r, 0)

            w_sent(shard, r, 2)

        @pl.when(z + k <= 3)
        def _():
            shard = d + 2 * k

            @pl.when(z > 0)
            def _():
                w_sent(shard, r, 1)

            w_sent(shard, r, 2)

    for off in range(1, ctx):
        shard = (d + off) % ctx
        w_sent(shard, r, 3)
        w_sent(shard, r, 4)
        w_sent(shard, x_peer, 4)


def fused_body(queries, key_rows, value_rows, doc_blocks, phm_mix, phm_blocks):
    ctx = 8
    any_space = pl.BlockSpec(memory_space=pl.ANY)
    smem = pl.BlockSpec(memory_space=pltpu.SMEM)
    cols_phm = phm_blocks.shape[1]
    return pl.pallas_call(
        fused_kernel,
        out_shape=jax.ShapeDtypeStruct((ROWS, PHM_N * cols_phm), jnp.bfloat16),
        in_specs=[smem, smem, any_space, any_space, any_space, any_space],
        out_specs=pl.BlockSpec(memory_space=pltpu.VMEM),
        scratch_shapes=[
            pltpu.VMEM((3, ctx, ROWS, HEAD_DIM), jnp.bfloat16),
            pltpu.VMEM((ctx, ROWS, HEAD_DIM), jnp.bfloat16),
            pltpu.VMEM((ctx, ROWS, HEAD_DIM), jnp.bfloat16),
            pltpu.VMEM((ctx, ROWS, cols_phm), jnp.bfloat16),
            pltpu.VMEM((PHM_N * ROWS, ctx * ROWS), jnp.bfloat16),
            pltpu.SemaphoreType.DMA((3, ctx)),
            pltpu.SemaphoreType.DMA((3, ctx)),
            pltpu.SemaphoreType.DMA((ctx,)),
            pltpu.SemaphoreType.DMA((ctx,)),
            pltpu.SemaphoreType.DMA((5, ctx, 4)),
            pltpu.SemaphoreType.DMA((ctx, 4)),
            pltpu.SemaphoreType.DMA,
        ],
        compiler_params=pltpu.CompilerParams(
            collective_id=0, has_side_effects=True, vmem_limit_bytes=40 * 1024 * 1024
        ),
        cost_estimate=pl.CostEstimate(
            flops=1_600_000_000, bytes_accessed=8_000_000, transcendentals=500_000
        ),
    )(doc_blocks, phm_mix.reshape(-1), queries, key_rows, value_rows, phm_blocks)


def either_body(sizes, *args):
    heads = args[0].shape[1] // HEAD_DIM
    if sizes == (8, 4) and heads == 8 and args[0].shape[0] == ROWS and args[5].shape[0] == ROWS:
        return fused_body(*args)
    return body(*args)


def solution(mesh):
    placed = (
        P(("rep", "ctx"), None),
        P(("rep", "ctx"), None),
        P(("rep", "ctx"), None),
        P("rep"),
        P(),
        P("ctx", None),
    )
    sizes = (mesh.shape["ctx"], mesh.shape["rep"])
    return jax.shard_map(
        functools.partial(either_body, sizes),
        mesh=mesh,
        in_specs=placed,
        out_specs=P(("rep", "ctx"), None),
        check_vma=False,
    )
```

```python
import functools
import math

import jax
import jax.numpy as jnp
from jax import lax
from jax.experimental import pallas as pl
from jax.experimental.pallas import tpu as pltpu
from jax.sharding import PartitionSpec as P

HEAD_DIM = 128
PHM_N = 4
UNIT = 128


def attend(q_all, k_all, v_all, doc_ids):
    seq_len = q_all.shape[0]
    block = min(512, seq_len)
    count = seq_len // block
    scale = 1.0 / math.sqrt(HEAD_DIM)
    heads_here = q_all.shape[1]

    def query_block(which):
        anchor = which * block
        q_part = lax.dynamic_slice_in_dim(q_all, anchor, block, 0)
        q_docs = lax.dynamic_slice_in_dim(doc_ids, anchor, block, 0)
        q_pos = anchor + jnp.arange(block, dtype=jnp.int32)
        lowest = jnp.int32(0)

        def key_block(kb, carry):
            running, total, accum = carry
            k_part = lax.dynamic_slice_in_dim(k_all, kb * block, block, 0)
            v_part = lax.dynamic_slice_in_dim(v_all, kb * block, block, 0)
            k_docs = lax.dynamic_slice_in_dim(doc_ids, kb * block, block, 0)
            k_pos = kb * block + jnp.arange(block, dtype=jnp.int32)
            allowed = (k_pos[None, :] <= q_pos[:, None]) & (k_docs[None, :] == q_docs[:, None])
            scores = (
                jnp.einsum("qhe,khe->hqk", q_part, k_part, preferred_element_type=jnp.float32)
                * scale
            )
            scores = jnp.where(allowed[None], scores, -1e30)
            newest = jnp.maximum(running, jnp.max(scores, axis=2))
            factor = jnp.exp(running - newest)
            expd = jnp.where(allowed[None], jnp.exp(scores - newest[:, :, None]), 0.0)
            total = total * factor + jnp.sum(expd, axis=2)
            update = jnp.einsum(
                "hqk,khe->hqe",
                expd.astype(jnp.bfloat16),
                v_part,
                preferred_element_type=jnp.float32,
            )
            accum = accum * factor[:, :, None] + update
            return (newest, total, accum)

        start_carry = (
            jnp.full((heads_here, block), -1e30, jnp.float32),
            jnp.zeros((heads_here, block), jnp.float32),
            jnp.zeros((heads_here, block, HEAD_DIM), jnp.float32),
        )
        running, total, accum = lax.fori_loop(lowest, which + 1, key_block, start_carry)
        result = (accum / total[:, :, None]).astype(jnp.bfloat16)
        return result.transpose(1, 0, 2)

    blocks_out = lax.map(query_block, jnp.arange(count, dtype=jnp.int32))
    return blocks_out.reshape(seq_len, heads_here, HEAD_DIM)


def body(queries, key_rows, value_rows, doc_blocks, phm_mix, phm_blocks):
    tok_rows = queries.shape[0]
    heads = queries.shape[1] // HEAD_DIM
    shaped = (
        queries.reshape(tok_rows, heads, HEAD_DIM),
        key_rows.reshape(tok_rows, heads, HEAD_DIM),
        value_rows.reshape(tok_rows, heads, HEAD_DIM),
    )
    q_all, k_all, v_all = (
        lax.all_to_all(shaped[0], "ctx", split_axis=1, concat_axis=0, tiled=True),
        lax.all_to_all(shaped[1], "ctx", split_axis=1, concat_axis=0, tiled=True),
        lax.all_to_all(shaped[2], "ctx", split_axis=1, concat_axis=0, tiled=True),
    )
    seq_len = q_all.shape[0]
    lengths = doc_blocks * UNIT
    docs = lengths.shape[0]
    upto = jnp.arange(docs)[None, :] <= jnp.arange(docs)[:, None]
    ends = jnp.sum(jnp.where(upto, lengths[None, :], 0), axis=1)
    positions = jnp.arange(seq_len, dtype=jnp.int32)
    doc_ids = jnp.sum((positions[:, None] >= ends[None, :]).astype(jnp.int32), axis=1)
    attended = attend(q_all, k_all, v_all, doc_ids)
    returned = lax.all_to_all(attended, "ctx", split_axis=0, concat_axis=1, tiled=True)
    rows_phm = heads * HEAD_DIM // PHM_N
    pieces = returned.reshape(tok_rows, PHM_N, rows_phm).astype(jnp.float32)
    mixed = jnp.einsum("iab,tar->tbir", phm_mix, pieces, precision=lax.Precision.HIGHEST)
    mixed = mixed.astype(jnp.bfloat16).reshape(tok_rows, PHM_N, PHM_N * rows_phm)
    cols_phm = phm_blocks.shape[1]
    output = jnp.einsum(
        "tbk,kc->tbc",
        mixed,
        lax.all_gather(phm_blocks, "ctx", axis=0, tiled=True),
        preferred_element_type=jnp.float32,
    )
    return output.reshape(tok_rows, PHM_N * cols_phm).astype(jnp.bfloat16)


MESH = pl.DeviceIdType.MESH
ROWS = UNIT
MASKED = -1e30


def fused_kernel(
    docs_ref, mix_ref, q_ref, k_ref, v_ref, w_ref, out_ref,
    qh, kv, obuf, att, wbuf, mixed,
    q_send, q_recv, kv_send, kv_recv, o_send, o_recv, w_send, w_recv, own_sem,
):
    ctx = 8
    window = 4
    d = lax.axis_index("ctx")
    r = lax.axis_index("rep")
    z = d // 2
    p = d % 2
    half_heads = 4
    half_cols = half_heads * HEAD_DIM
    y_peer = d + 1 - 2 * (d % 2)
    x_peer = (r + 2) % 4
    c_peer = r + 1 - 2 * (r % 2)
    part = ROWS // 4

    barrier = pltpu.get_barrier_semaphore()

    def greet(target):
        pl.semaphore_signal(barrier, inc=1, device_id=target, device_id_type=MESH)

    greet({"ctx": y_peer})
    greet({"rep": x_peer})
    greet({"rep": c_peer})

    @pl.when(z < 3)
    def _():
        greet({"ctx": d + 2})

    @pl.when(z > 0)
    def _():
        greet({"ctx": d - 2})

    pl.semaphore_wait(barrier, 4 + jnp.where((z > 0) & (z < 3), 1, 0))

    def quarter(shard, which):
        return wbuf.at[shard, pl.ds(pl.multiple_of(which * part, part), part)]

    def w_copy(src, shard, which, way, target):
        return pltpu.make_async_remote_copy(
            src_ref=src,
            dst_ref=quarter(shard, which),
            send_sem=w_send.at[way, shard, which],
            recv_sem=w_recv.at[shard, which],
            device_id=target,
            device_id_type=MESH,
        )

    def w_arrived(shard, which):
        here = quarter(shard, which)
        pltpu.make_async_copy(here, here, w_recv.at[shard, which]).wait()

    def w_sent(shard, which, way):
        here = quarter(shard, which)
        pltpu.make_async_copy(here, here, w_send.at[way, shard, which]).wait()

    own_w = w_ref.at[pl.ds(pl.multiple_of(r * part, part), part)]

    refs = (k_ref, v_ref)

    def half_of(ref, which):
        return ref.at[:, pl.ds(pl.multiple_of(which * half_cols, half_cols), half_cols)]

    def remote(src, dst, send, recv, to):
        return pltpu.make_async_remote_copy(
            src_ref=src, dst_ref=dst, send_sem=send, recv_sem=recv,
            device_id={"ctx": to}, device_id_type=MESH,
        )

    def kv_partner(j):
        return remote(
            half_of(refs[j], 1 - p), kv.at[j, 3 + p], kv_send.at[j, 0], kv_recv.at[j, 3 + p], y_peer
        )

    def kv_up(j):
        return remote(
            half_of(refs[j], p), kv.at[j, 1 + p], kv_send.at[j, 1], kv_recv.at[j, 1 + p], d + 2
        )

    def kv_relay(j):
        return remote(
            kv.at[j, 4 - p], kv.at[j, 2 - p], kv_send.at[j, 2], kv_recv.at[j, 2 - p], d + 2
        )

    def kv_far(j):
        return remote(kv.at[j, 2], kv.at[j, 0], kv_send.at[j, 3], kv_recv.at[j, 0], d + 2)

    def kv_here(j, slot):
        here = kv.at[j, slot]
        pltpu.make_async_copy(here, here, kv_recv.at[j, slot]).wait()

    q_partner = remote(half_of(q_ref, 1 - p), qh.at[p], q_send, q_recv.at[p], y_peer)
    for j in range(2):
        kv_partner(j).start()

    @pl.when(z < 3)
    def _():
        for j in range(2):
            kv_up(j).start()

    @pl.when(z < 3)
    def _():
        w_copy(own_w, d, r, 0, {"ctx": d + 2}).start()

    @pl.when(z > 0)
    def _():
        w_copy(own_w, d, r, 1, {"ctx": d - 2}).start()

    w_copy(own_w, d, r, 2, {"ctx": y_peer}).start()

    for j in range(2):
        pltpu.make_async_copy(half_of(refs[j], p), kv.at[j, 3 + p], kv_recv.at[j, 3 + p]).start()
    q_partner.start()
    pltpu.make_async_copy(half_of(q_ref, p), qh.at[p], q_recv.at[p]).start()
    own_copy = pltpu.make_async_copy(w_ref, wbuf.at[d], own_sem)
    own_copy.start()

    @pl.when(z < 1)
    def _():
        kv[:, 1:3] = jnp.zeros((2, 2, ROWS, half_cols), jnp.bfloat16)

    @pl.when(z < 2)
    def _():
        kv[:, 0:1] = jnp.zeros((2, 1, ROWS, half_cols), jnp.bfloat16)

    def forward(shard, which, way, target):
        w_copy(quarter(shard, which), shard, which, way, target).start()

    for k in range(1, 4):

        @pl.when(z - k >= 0)
        def _():
            shard = d - 2 * k
            w_arrived(shard, r)

            @pl.when(z < 3)
            def _():
                forward(shard, r, 0, {"ctx": d + 2})

            forward(shard, r, 2, {"ctx": y_peer})
            forward(shard, r, 3, {"rep": x_peer})
            forward(shard, r, 4, {"rep": c_peer})

        @pl.when(z + k <= 3)
        def _():
            shard = d + 2 * k
            w_arrived(shard, r)

            @pl.when(z > 0)
            def _():
                forward(shard, r, 1, {"ctx": d - 2})

            forward(shard, r, 2, {"ctx": y_peer})
            forward(shard, r, 3, {"rep": x_peer})
            forward(shard, r, 4, {"rep": c_peer})

    for j in range(2):
        kv_here(j, 3)
        kv_here(j, 4)

        @pl.when(z < 3)
        def _():
            kv_relay(j).start()

    for j in range(2):

        @pl.when(z > 0)
        def _():
            kv_here(j, 2)

        @pl.when((z > 0) & (z < 3))
        def _():
            kv_far(j).start()

    for k in range(4):
        shard = (y_peer + 2 * k) % ctx
        w_arrived(shard, r)
        forward(shard, r, 3, {"rep": x_peer})
        forward(shard, r, 4, {"rep": c_peer})

    ends = [docs_ref[0]]
    for i in range(1, docs_ref.shape[0]):
        ends.append(ends[-1] + docs_ref[i])
    factor = math.log2(math.e) / math.sqrt(HEAD_DIM)
    rows = lax.broadcasted_iota(jnp.int32, (ROWS, ROWS), 0)
    cols = lax.broadcasted_iota(jnp.int32, (ROWS, ROWS), 1)

    def doc_of(b):
        doc = jnp.int32(0)
        for e in ends:
            doc = doc + jnp.where(e <= b, jnp.int32(1), jnp.int32(0))
        return doc

    for j in range(2):

        @pl.when(z > 0)
        def _():
            kv_here(j, 1)

        @pl.when(z > 1)
        def _():
            kv_here(j, 0)

    for par in range(2):
        here = qh.at[par]
        pltpu.make_async_copy(here, here, q_recv.at[par]).wait()

    o_copy = remote(obuf, att.at[pl.ds(half_heads * p, half_heads)], o_send, o_recv, y_peer)
    wide = window * ROWS
    for par, own in ((1 - p, False), (p, True)):
        block = 2 * z + par
        doc = doc_of(block)
        bias = []
        for i in range(window - 1):
            b = block - (window - 1) + i
            bias.append(jnp.where((b >= 0) & (doc_of(b) == doc), 0.0, MASKED))
        for h in range(half_heads):
            lanes = slice(h * HEAD_DIM, (h + 1) * HEAD_DIM)
            keys = kv[0, pl.ds(par, window), :, lanes].reshape(wide, HEAD_DIM)
            vals = kv[1, pl.ds(par, window), :, lanes].reshape(wide, HEAD_DIM)
            scores = lax.dot_general(
                qh[par, :, lanes], keys, (((1,), (1,)), ((), ())),
                preferred_element_type=jnp.float32,
            )
            parts = [scores[:, i * ROWS : (i + 1) * ROWS] + bias[i] for i in range(window - 1)]
            parts.append(jnp.where(cols <= rows, scores[:, (window - 1) * ROWS :], MASKED))
            masked = jnp.concatenate(parts, axis=1)
            top = jnp.max(masked, axis=1, keepdims=True)
            expd = jnp.exp2((masked - top) * factor)
            total = jnp.sum(expd, axis=1, keepdims=True)
            got = jnp.dot(expd.astype(jnp.bfloat16), vals, preferred_element_type=jnp.float32)
            got = (got / total).astype(jnp.bfloat16)
            if own:
                att[half_heads * p + h] = got
            else:
                obuf[h] = got
        if not own:
            o_copy.start()

    for off in range(1, ctx):
        shard = (d + off) % ctx
        w_arrived(shard, x_peer)
        forward(shard, x_peer, 4, {"rep": c_peer})

    o_copy.wait_recv()

    for half in range(2):
        pieces = [att[2 * a + half].astype(jnp.float32) for a in range(PHM_N)]
        for i in range(PHM_N):
            for b in range(PHM_N):
                acc = mix_ref[i, 0, b] * pieces[0]
                for a in range(1, PHM_N):
                    acc = acc + mix_ref[i, a, b] * pieces[a]
                lo = i * 2 * HEAD_DIM + half * HEAD_DIM
                mixed[b * ROWS : (b + 1) * ROWS, lo : lo + HEAD_DIM] = acc.astype(jnp.bfloat16)

    own_copy.wait()
    x_of_c = (c_peer + 2) % 4
    for off in range(1, ctx):
        shard = (d + off) % ctx
        w_arrived(shard, c_peer)
        w_arrived(shard, x_of_c)

    cols_phm = w_ref.shape[1]
    tile = 256
    for c in range(cols_phm // tile):
        weights = wbuf[:, :, c * tile : (c + 1) * tile].reshape(ctx * ROWS, tile)
        res = jnp.dot(mixed[...], weights, preferred_element_type=jnp.float32)
        res = res.astype(jnp.bfloat16)
        for b in range(PHM_N):
            at = b * cols_phm + c * tile
            out_ref[:, at : at + tile] = res[b * ROWS : (b + 1) * ROWS]

    q_partner.wait_send()
    o_copy.wait_send()
    for j in range(2):
        kv_partner(j).wait_send()

        @pl.when(z < 3)
        def _():
            kv_up(j).wait_send()
            kv_relay(j).wait_send()

        @pl.when((z > 0) & (z < 3))
        def _():
            kv_far(j).wait_send()

    @pl.when(z < 3)
    def _():
        w_sent(d, r, 0)

    @pl.when(z > 0)
    def _():
        w_sent(d, r, 1)

    w_sent(d, r, 2)
    for k in range(1, 4):

        @pl.when(z - k >= 0)
        def _():
            shard = d - 2 * k

            @pl.when(z < 3)
            def _():
                w_sent(shard, r, 0)

            w_sent(shard, r, 2)

        @pl.when(z + k <= 3)
        def _():
            shard = d + 2 * k

            @pl.when(z > 0)
            def _():
                w_sent(shard, r, 1)

            w_sent(shard, r, 2)

    for off in range(1, ctx):
        shard = (d + off) % ctx
        w_sent(shard, r, 3)
        w_sent(shard, r, 4)
        w_sent(shard, x_peer, 4)


def fused_body(queries, key_rows, value_rows, doc_blocks, phm_mix, phm_blocks):
    ctx = 8
    any_space = pl.BlockSpec(memory_space=pl.ANY)
    smem = pl.BlockSpec(memory_space=pltpu.SMEM)
    cols_phm = phm_blocks.shape[1]
    return pl.pallas_call(
        fused_kernel,
        out_shape=jax.ShapeDtypeStruct((ROWS, PHM_N * cols_phm), jnp.bfloat16),
        in_specs=[smem, smem, any_space, any_space, any_space, any_space],
        out_specs=pl.BlockSpec(memory_space=pltpu.VMEM),
        scratch_shapes=[
            pltpu.VMEM((2, ROWS, 4 * HEAD_DIM), jnp.bfloat16),
            pltpu.VMEM((2, 5, ROWS, 4 * HEAD_DIM), jnp.bfloat16),
            pltpu.VMEM((4, ROWS, HEAD_DIM), jnp.bfloat16),
            pltpu.VMEM((ctx, ROWS, HEAD_DIM), jnp.bfloat16),
            pltpu.VMEM((ctx, ROWS, cols_phm), jnp.bfloat16),
            pltpu.VMEM((PHM_N * ROWS, ctx * ROWS), jnp.bfloat16),
            pltpu.SemaphoreType.DMA,
            pltpu.SemaphoreType.DMA((2,)),
            pltpu.SemaphoreType.DMA((2, 4)),
            pltpu.SemaphoreType.DMA((2, 5)),
            pltpu.SemaphoreType.DMA,
            pltpu.SemaphoreType.DMA,
            pltpu.SemaphoreType.DMA((5, ctx, 4)),
            pltpu.SemaphoreType.DMA((ctx, 4)),
            pltpu.SemaphoreType.DMA,
        ],
        compiler_params=pltpu.CompilerParams(
            collective_id=0, has_side_effects=True, vmem_limit_bytes=60 * 1024 * 1024
        ),
        cost_estimate=pl.CostEstimate(
            flops=1_600_000_000, bytes_accessed=8_000_000, transcendentals=500_000
        ),
    )(doc_blocks, phm_mix, queries, key_rows, value_rows, phm_blocks)


def either_body(sizes, *args):
    heads = args[0].shape[1] // HEAD_DIM
    if sizes == (8, 4) and heads == 8 and args[0].shape[0] == ROWS and args[5].shape[0] == ROWS:
        return fused_body(*args)
    return body(*args)


def solution(mesh):
    placed = (
        P(("rep", "ctx"), None),
        P(("rep", "ctx"), None),
        P(("rep", "ctx"), None),
        P("rep"),
        P(),
        P("ctx", None),
    )
    sizes = (mesh.shape["ctx"], mesh.shape["rep"])
    return jax.shard_map(
        functools.partial(either_body, sizes),
        mesh=mesh,
        in_specs=placed,
        out_specs=P(("rep", "ctx"), None),
        check_vma=False,
    )
```

```python
import functools
import math

import jax
import jax.numpy as jnp
from jax import lax
from jax.experimental import pallas as pl
from jax.experimental.pallas import tpu as pltpu
from jax.sharding import PartitionSpec as P

HEAD_DIM = 128
PHM_N = 4
UNIT = 128


def attend(q_all, k_all, v_all, doc_ids):
    seq_len = q_all.shape[0]
    block = min(512, seq_len)
    count = seq_len // block
    scale = 1.0 / math.sqrt(HEAD_DIM)
    heads_here = q_all.shape[1]

    def query_block(which):
        anchor = which * block
        q_part = lax.dynamic_slice_in_dim(q_all, anchor, block, 0)
        q_docs = lax.dynamic_slice_in_dim(doc_ids, anchor, block, 0)
        q_pos = anchor + jnp.arange(block, dtype=jnp.int32)
        lowest = jnp.int32(0)

        def key_block(kb, carry):
            running, total, accum = carry
            k_part = lax.dynamic_slice_in_dim(k_all, kb * block, block, 0)
            v_part = lax.dynamic_slice_in_dim(v_all, kb * block, block, 0)
            k_docs = lax.dynamic_slice_in_dim(doc_ids, kb * block, block, 0)
            k_pos = kb * block + jnp.arange(block, dtype=jnp.int32)
            allowed = (k_pos[None, :] <= q_pos[:, None]) & (k_docs[None, :] == q_docs[:, None])
            scores = (
                jnp.einsum("qhe,khe->hqk", q_part, k_part, preferred_element_type=jnp.float32)
                * scale
            )
            scores = jnp.where(allowed[None], scores, -1e30)
            newest = jnp.maximum(running, jnp.max(scores, axis=2))
            factor = jnp.exp(running - newest)
            expd = jnp.where(allowed[None], jnp.exp(scores - newest[:, :, None]), 0.0)
            total = total * factor + jnp.sum(expd, axis=2)
            update = jnp.einsum(
                "hqk,khe->hqe",
                expd.astype(jnp.bfloat16),
                v_part,
                preferred_element_type=jnp.float32,
            )
            accum = accum * factor[:, :, None] + update
            return (newest, total, accum)

        start_carry = (
            jnp.full((heads_here, block), -1e30, jnp.float32),
            jnp.zeros((heads_here, block), jnp.float32),
            jnp.zeros((heads_here, block, HEAD_DIM), jnp.float32),
        )
        running, total, accum = lax.fori_loop(lowest, which + 1, key_block, start_carry)
        result = (accum / total[:, :, None]).astype(jnp.bfloat16)
        return result.transpose(1, 0, 2)

    blocks_out = lax.map(query_block, jnp.arange(count, dtype=jnp.int32))
    return blocks_out.reshape(seq_len, heads_here, HEAD_DIM)


def body(queries, key_rows, value_rows, doc_blocks, phm_mix, phm_blocks):
    tok_rows = queries.shape[0]
    heads = queries.shape[1] // HEAD_DIM
    shaped = (
        queries.reshape(tok_rows, heads, HEAD_DIM),
        key_rows.reshape(tok_rows, heads, HEAD_DIM),
        value_rows.reshape(tok_rows, heads, HEAD_DIM),
    )
    q_all, k_all, v_all = (
        lax.all_to_all(shaped[0], "ctx", split_axis=1, concat_axis=0, tiled=True),
        lax.all_to_all(shaped[1], "ctx", split_axis=1, concat_axis=0, tiled=True),
        lax.all_to_all(shaped[2], "ctx", split_axis=1, concat_axis=0, tiled=True),
    )
    seq_len = q_all.shape[0]
    lengths = doc_blocks * UNIT
    docs = lengths.shape[0]
    upto = jnp.arange(docs)[None, :] <= jnp.arange(docs)[:, None]
    ends = jnp.sum(jnp.where(upto, lengths[None, :], 0), axis=1)
    positions = jnp.arange(seq_len, dtype=jnp.int32)
    doc_ids = jnp.sum((positions[:, None] >= ends[None, :]).astype(jnp.int32), axis=1)
    attended = attend(q_all, k_all, v_all, doc_ids)
    returned = lax.all_to_all(attended, "ctx", split_axis=0, concat_axis=1, tiled=True)
    rows_phm = heads * HEAD_DIM // PHM_N
    pieces = returned.reshape(tok_rows, PHM_N, rows_phm).astype(jnp.float32)
    mixed = jnp.einsum("iab,tar->tbir", phm_mix, pieces, precision=lax.Precision.HIGHEST)
    mixed = mixed.astype(jnp.bfloat16).reshape(tok_rows, PHM_N, PHM_N * rows_phm)
    cols_phm = phm_blocks.shape[1]
    output = jnp.einsum(
        "tbk,kc->tbc",
        mixed,
        lax.all_gather(phm_blocks, "ctx", axis=0, tiled=True),
        preferred_element_type=jnp.float32,
    )
    return output.reshape(tok_rows, PHM_N * cols_phm).astype(jnp.bfloat16)


MESH = pl.DeviceIdType.MESH
ROWS = UNIT
MASKED = -1e30


def fused_kernel(
    docs_ref, mix_ref, q_ref, k_ref, v_ref, w_ref, out_ref,
    qh, kv, obuf, att, wbuf, mixed,
    q_send, q_recv, kv_send, kv_recv, o_send, o_recv, w_send, w_recv, own_sem,
):
    ctx = 8
    window = 4
    d = lax.axis_index("ctx")
    r = lax.axis_index("rep")
    z = d // 2
    p = d % 2
    half_heads = 4
    half_cols = half_heads * HEAD_DIM
    y_peer = d + 1 - 2 * (d % 2)
    x_peer = (r + 2) % 4
    c_peer = r + 1 - 2 * (r % 2)
    part = ROWS // 4

    barrier = pltpu.get_barrier_semaphore()

    def greet(target):
        pl.semaphore_signal(barrier, inc=1, device_id=target, device_id_type=MESH)

    greet({"ctx": y_peer})
    greet({"rep": x_peer})
    greet({"rep": c_peer})

    @pl.when(z < 3)
    def _():
        greet({"ctx": d + 2})

    @pl.when(z > 0)
    def _():
        greet({"ctx": d - 2})

    pl.semaphore_wait(barrier, 4 + jnp.where((z > 0) & (z < 3), 1, 0))

    def quarter(shard, which):
        return wbuf.at[shard, pl.ds(pl.multiple_of(which * part, part), part)]

    def w_copy(src, shard, which, way, target):
        return pltpu.make_async_remote_copy(
            src_ref=src,
            dst_ref=quarter(shard, which),
            send_sem=w_send.at[way, shard, which],
            recv_sem=w_recv.at[shard, which],
            device_id=target,
            device_id_type=MESH,
        )

    def w_arrived(shard, which):
        here = quarter(shard, which)
        pltpu.make_async_copy(here, here, w_recv.at[shard, which]).wait()

    def w_sent(shard, which, way):
        here = quarter(shard, which)
        pltpu.make_async_copy(here, here, w_send.at[way, shard, which]).wait()

    own_w = w_ref.at[pl.ds(pl.multiple_of(r * part, part), part)]

    refs = (k_ref, v_ref)

    def half_of(ref, which):
        return ref.at[:, pl.ds(pl.multiple_of(which * half_cols, half_cols), half_cols)]

    def remote(src, dst, send, recv, to):
        return pltpu.make_async_remote_copy(
            src_ref=src, dst_ref=dst, send_sem=send, recv_sem=recv,
            device_id={"ctx": to}, device_id_type=MESH,
        )

    def kv_partner(j):
        return remote(
            half_of(refs[j], 1 - p), kv.at[j, 3 + p], kv_send.at[j, 0], kv_recv.at[j, 3 + p], y_peer
        )

    def kv_up(j):
        return remote(
            half_of(refs[j], p), kv.at[j, 1 + p], kv_send.at[j, 1], kv_recv.at[j, 1 + p], d + 2
        )

    def kv_relay(j):
        return remote(
            kv.at[j, 4 - p], kv.at[j, 2 - p], kv_send.at[j, 2], kv_recv.at[j, 2 - p], d + 2
        )

    def kv_far(j):
        return remote(kv.at[j, 2], kv.at[j, 0], kv_send.at[j, 3], kv_recv.at[j, 0], d + 2)

    def kv_here(j, slot):
        here = kv.at[j, slot]
        pltpu.make_async_copy(here, here, kv_recv.at[j, slot]).wait()

    q_partner = remote(half_of(q_ref, 1 - p), qh.at[p], q_send, q_recv.at[p], y_peer)
    @pl.when(z < 3)
    def _():
        w_copy(own_w, d, r, 0, {"ctx": d + 2}).start()

    @pl.when(z > 0)
    def _():
        w_copy(own_w, d, r, 1, {"ctx": d - 2}).start()

    w_copy(own_w, d, r, 2, {"ctx": y_peer}).start()

    for j in range(2):
        kv_partner(j).start()

    @pl.when(z < 3)
    def _():
        for j in range(2):
            kv_up(j).start()

    for j in range(2):
        pltpu.make_async_copy(half_of(refs[j], p), kv.at[j, 3 + p], kv_recv.at[j, 3 + p]).start()
    q_partner.start()
    pltpu.make_async_copy(half_of(q_ref, p), qh.at[p], q_recv.at[p]).start()
    own_copy = pltpu.make_async_copy(w_ref, wbuf.at[d], own_sem)
    own_copy.start()

    @pl.when(z < 1)
    def _():
        kv[:, 1:3] = jnp.zeros((2, 2, ROWS, half_cols), jnp.bfloat16)

    @pl.when(z < 2)
    def _():
        kv[:, 0:1] = jnp.zeros((2, 1, ROWS, half_cols), jnp.bfloat16)

    def forward(shard, which, way, target):
        w_copy(quarter(shard, which), shard, which, way, target).start()

    for k in range(1, 4):

        @pl.when(z - k >= 0)
        def _():
            shard = d - 2 * k
            w_arrived(shard, r)

            @pl.when(z < 3)
            def _():
                forward(shard, r, 0, {"ctx": d + 2})

            forward(shard, r, 2, {"ctx": y_peer})
            forward(shard, r, 3, {"rep": x_peer})
            forward(shard, r, 4, {"rep": c_peer})

        @pl.when(z + k <= 3)
        def _():
            shard = d + 2 * k
            w_arrived(shard, r)

            @pl.when(z > 0)
            def _():
                forward(shard, r, 1, {"ctx": d - 2})

            forward(shard, r, 2, {"ctx": y_peer})
            forward(shard, r, 3, {"rep": x_peer})
            forward(shard, r, 4, {"rep": c_peer})

    for j in range(2):
        kv_here(j, 3)
        kv_here(j, 4)

        @pl.when(z < 3)
        def _():
            kv_relay(j).start()

    for j in range(2):

        @pl.when(z > 0)
        def _():
            kv_here(j, 2)

        @pl.when((z > 0) & (z < 3))
        def _():
            kv_far(j).start()

    for k in range(4):
        shard = (y_peer + 2 * k) % ctx
        w_arrived(shard, r)
        forward(shard, r, 3, {"rep": x_peer})
        forward(shard, r, 4, {"rep": c_peer})

    ends = [docs_ref[0]]
    for i in range(1, docs_ref.shape[0]):
        ends.append(ends[-1] + docs_ref[i])
    factor = math.log2(math.e) / math.sqrt(HEAD_DIM)
    rows = lax.broadcasted_iota(jnp.int32, (ROWS, ROWS), 0)
    cols = lax.broadcasted_iota(jnp.int32, (ROWS, ROWS), 1)

    def doc_of(b):
        doc = jnp.int32(0)
        for e in ends:
            doc = doc + jnp.where(e <= b, jnp.int32(1), jnp.int32(0))
        return doc

    for j in range(2):

        @pl.when(z > 0)
        def _():
            kv_here(j, 1)

        @pl.when(z > 1)
        def _():
            kv_here(j, 0)

    for par in range(2):
        here = qh.at[par]
        pltpu.make_async_copy(here, here, q_recv.at[par]).wait()

    o_copy = remote(obuf, att.at[pl.ds(half_heads * p, half_heads)], o_send, o_recv, y_peer)
    wide = window * ROWS
    for par, own in ((1 - p, False), (p, True)):
        block = 2 * z + par
        doc = doc_of(block)
        bias = []
        for i in range(window - 1):
            b = block - (window - 1) + i
            bias.append(jnp.where((b >= 0) & (doc_of(b) == doc), 0.0, MASKED))
        for h in range(half_heads):
            lanes = slice(h * HEAD_DIM, (h + 1) * HEAD_DIM)
            keys = kv[0, pl.ds(par, window), :, lanes].reshape(wide, HEAD_DIM)
            vals = kv[1, pl.ds(par, window), :, lanes].reshape(wide, HEAD_DIM)
            scores = lax.dot_general(
                qh[par, :, lanes], keys, (((1,), (1,)), ((), ())),
                preferred_element_type=jnp.float32,
            )
            parts = [scores[:, i * ROWS : (i + 1) * ROWS] + bias[i] for i in range(window - 1)]
            parts.append(jnp.where(cols <= rows, scores[:, (window - 1) * ROWS :], MASKED))
            masked = jnp.concatenate(parts, axis=1)
            top = jnp.max(masked, axis=1, keepdims=True)
            expd = jnp.exp2((masked - top) * factor)
            total = jnp.sum(expd, axis=1, keepdims=True)
            got = jnp.dot(expd.astype(jnp.bfloat16), vals, preferred_element_type=jnp.float32)
            got = (got / total).astype(jnp.bfloat16)
            if own:
                att[half_heads * p + h] = got
            else:
                obuf[h] = got
        if not own:
            o_copy.start()

    for off in range(1, ctx):
        shard = (d + off) % ctx
        w_arrived(shard, x_peer)
        forward(shard, x_peer, 4, {"rep": c_peer})

    o_copy.wait_recv()

    for half in range(2):
        pieces = [att[2 * a + half].astype(jnp.float32) for a in range(PHM_N)]
        for i in range(PHM_N):
            for b in range(PHM_N):
                acc = mix_ref[i, 0, b] * pieces[0]
                for a in range(1, PHM_N):
                    acc = acc + mix_ref[i, a, b] * pieces[a]
                lo = i * 2 * HEAD_DIM + half * HEAD_DIM
                mixed[b * ROWS : (b + 1) * ROWS, lo : lo + HEAD_DIM] = acc.astype(jnp.bfloat16)

    own_copy.wait()
    x_of_c = (c_peer + 2) % 4
    for off in range(1, ctx):
        shard = (d + off) % ctx
        w_arrived(shard, c_peer)
        w_arrived(shard, x_of_c)

    cols_phm = w_ref.shape[1]
    tile = 256
    for c in range(cols_phm // tile):
        weights = wbuf[:, :, c * tile : (c + 1) * tile].reshape(ctx * ROWS, tile)
        res = jnp.dot(mixed[...], weights, preferred_element_type=jnp.float32)
        res = res.astype(jnp.bfloat16)
        for b in range(PHM_N):
            at = b * cols_phm + c * tile
            out_ref[:, at : at + tile] = res[b * ROWS : (b + 1) * ROWS]

    q_partner.wait_send()
    o_copy.wait_send()
    for j in range(2):
        kv_partner(j).wait_send()

        @pl.when(z < 3)
        def _():
            kv_up(j).wait_send()
            kv_relay(j).wait_send()

        @pl.when((z > 0) & (z < 3))
        def _():
            kv_far(j).wait_send()

    @pl.when(z < 3)
    def _():
        w_sent(d, r, 0)

    @pl.when(z > 0)
    def _():
        w_sent(d, r, 1)

    w_sent(d, r, 2)
    for k in range(1, 4):

        @pl.when(z - k >= 0)
        def _():
            shard = d - 2 * k

            @pl.when(z < 3)
            def _():
                w_sent(shard, r, 0)

            w_sent(shard, r, 2)

        @pl.when(z + k <= 3)
        def _():
            shard = d + 2 * k

            @pl.when(z > 0)
            def _():
                w_sent(shard, r, 1)

            w_sent(shard, r, 2)

    for off in range(1, ctx):
        shard = (d + off) % ctx
        w_sent(shard, r, 3)
        w_sent(shard, r, 4)
        w_sent(shard, x_peer, 4)


def fused_body(queries, key_rows, value_rows, doc_blocks, phm_mix, phm_blocks):
    ctx = 8
    any_space = pl.BlockSpec(memory_space=pl.ANY)
    smem = pl.BlockSpec(memory_space=pltpu.SMEM)
    cols_phm = phm_blocks.shape[1]
    return pl.pallas_call(
        fused_kernel,
        out_shape=jax.ShapeDtypeStruct((ROWS, PHM_N * cols_phm), jnp.bfloat16),
        in_specs=[smem, smem, any_space, any_space, any_space, any_space],
        out_specs=pl.BlockSpec(memory_space=pltpu.VMEM),
        scratch_shapes=[
            pltpu.VMEM((2, ROWS, 4 * HEAD_DIM), jnp.bfloat16),
            pltpu.VMEM((2, 5, ROWS, 4 * HEAD_DIM), jnp.bfloat16),
            pltpu.VMEM((4, ROWS, HEAD_DIM), jnp.bfloat16),
            pltpu.VMEM((ctx, ROWS, HEAD_DIM), jnp.bfloat16),
            pltpu.VMEM((ctx, ROWS, cols_phm), jnp.bfloat16),
            pltpu.VMEM((PHM_N * ROWS, ctx * ROWS), jnp.bfloat16),
            pltpu.SemaphoreType.DMA,
            pltpu.SemaphoreType.DMA((2,)),
            pltpu.SemaphoreType.DMA((2, 4)),
            pltpu.SemaphoreType.DMA((2, 5)),
            pltpu.SemaphoreType.DMA,
            pltpu.SemaphoreType.DMA,
            pltpu.SemaphoreType.DMA((5, ctx, 4)),
            pltpu.SemaphoreType.DMA((ctx, 4)),
            pltpu.SemaphoreType.DMA,
        ],
        compiler_params=pltpu.CompilerParams(
            collective_id=0, has_side_effects=True, vmem_limit_bytes=60 * 1024 * 1024
        ),
        cost_estimate=pl.CostEstimate(
            flops=1_600_000_000, bytes_accessed=8_000_000, transcendentals=500_000
        ),
    )(doc_blocks, phm_mix, queries, key_rows, value_rows, phm_blocks)


def either_body(sizes, *args):
    heads = args[0].shape[1] // HEAD_DIM
    if sizes == (8, 4) and heads == 8 and args[0].shape[0] == ROWS and args[5].shape[0] == ROWS:
        return fused_body(*args)
    return body(*args)


def solution(mesh):
    placed = (
        P(("rep", "ctx"), None),
        P(("rep", "ctx"), None),
        P(("rep", "ctx"), None),
        P("rep"),
        P(),
        P("ctx", None),
    )
    sizes = (mesh.shape["ctx"], mesh.shape["rep"])
    return jax.shard_map(
        functools.partial(either_body, sizes),
        mesh=mesh,
        in_specs=placed,
        out_specs=P(("rep", "ctx"), None),
        check_vma=False,
    )
```
